32 devices in a mesh: groups: 2 (over y), tensor: 4 (over z), dp: 4 (over x, core).
Axes of the slice: x: 2, y: 2, z: 4, core: 2. Of those that a mesh axis runs over, the one named last changes fastest.
Arguments:
- cotangent: bfloat16 [4, 1024, 2560], P('dp', ('groups', 'tensor')), parts along dimension 1, may hold values from -6 to 6
- gate_pre: bfloat16 [4096, 12800], P(('groups', 'dp'), 'tensor'), parts along dimension 0, may hold values from -8 to 8
- up_pre: bfloat16 [4096, 12800], P(('groups', 'dp'), 'tensor'), parts along dimension 0, may hold values from -6 to 6
- down_weight: bfloat16 [12800, 2560], P('tensor'), may hold values from -0.0546875 to 0.0546875
- adapter_in: bfloat16 [256, 16, 12800], P(('groups', 'dp'), None, 'tensor'), parts along dimension 0, may hold values from -0.19921875 to 0.19921875
- adapter_out: bfloat16 [256, 16, 2560], P(('groups', 'dp'), None, 'tensor'), parts along dimension 0, may hold values from -0.125 to 0.125
- token_adapter: int32 [4096], P('groups'), parts along dimension 0, may hold values from 0 to 127, as said below
- live_rows: int32 [32], P('groups'), parts along dimension 0, may hold values from 1 to 128, as said below
- adapter_slot: int32 [256], P('groups'), parts along dimension 0, may hold values from 0 to 127, as said below
Outputs:
- gate_grad: bfloat16 [4096, 12800], P(('groups', 'dp'), 'tensor'), parts along dimension 0
- up_grad: bfloat16 [4096, 12800], P(('groups', 'dp'), 'tensor'), parts along dimension 0
- grad_in: bfloat16 [256, 16, 12800], P(('groups', 'dp'), None, 'tensor'), parts along dimension 0
- grad_out: bfloat16 [256, 16, 2560], P(('groups', 'dp'), None, 'tensor'), parts along dimension 0
The draws below stay inside these ranges and needn't reach their ends.
There are 2 independent parts, one for each index of `groups`. The reference program is written for one: setup_inputs(seed, part) draws one part's arguments, and reference() takes and returns one part's arrays. A program takes and returns all parts, laid end to end along the dimension named above; an argument that names none is the same for every part. Nothing has to cross between parts.
Inputs may be any that keep to these rules, and one draw needn't show every extreme that they name: `token_adapter`: the 128 rows of each aligned block share one adapter id; among the blocks of one dp index (rows of 512), at most 1 use adapters whose slots belong to any one owner, and exactly 1 for some owner. In each block the first live_rows rows carry tokens and the rest are padding; some block is full. `adapter_slot`: a permutation of the slots.
All inputs are finite; a program needn't handle non-finite values.
Results may differ from the reference program's by a relative error of at most 0.0057.
Values may be sent and summed in bfloat16 or wider, within the bound.
A program may use at most 128 MiB of HBM per device.

```python
import jax
import jax.numpy as jnp

D = 2560
FF = 12800
RANK = 16
ADP_DEV = 32
BLOCK = 128
TOK_DEV = 512
ADAPTERS = 128
TOKENS = 2048
NBLK = 16
DPS = 4
N_DP = 4


def shared_slots(key):
    return jax.random.permutation(jax.random.fold_in(key, 7), ADAPTERS).astype(jnp.int32)


def draw_adapter_slot(key, part):
    return shared_slots(key)


def draw_token_adapter(key, part):
    order = shared_slots(key)
    key = jax.random.fold_in(key, 11)
    first_key, second_key, third_key = jax.random.split(key, 3)
    blocks = TOK_DEV // BLOCK
    owner_keys = jax.random.split(first_key, N_DP)
    owner_perm = jax.vmap(lambda k: jax.random.permutation(k, N_DP))(owner_keys)
    column = jnp.arange(blocks, dtype=jnp.int32) % N_DP
    owners = owner_perm[:, column].astype(jnp.int32)
    first = jax.random.randint(second_key, (N_DP, blocks), 0, ADP_DEV)
    second = jax.random.randint(third_key, (N_DP, blocks), 0, ADP_DEV)
    local = jnp.minimum(first, second)
    slot_grid = owners * ADP_DEV + local
    inverse = jnp.argsort(order).astype(jnp.int32)
    chosen = inverse[slot_grid.reshape(-1)]
    return jnp.repeat(chosen, BLOCK, total_repeat_length=TOKENS).astype(jnp.int32)


def draw_live_rows(key, part):
    key = jax.random.fold_in(key, 12)
    first_key, second_key = jax.random.split(key, 2)
    counts = jax.random.randint(first_key, (TOKENS // BLOCK,), 1, BLOCK + 1)
    chosen = jax.random.randint(second_key, (), 0, TOKENS // BLOCK)
    filled = jnp.where(jnp.arange(TOKENS // BLOCK) == chosen, BLOCK, counts)
    return filled.astype(jnp.int32)


def levels(own_key, dims, shards, least, high):
    gain = 1.0
    for dim, shards_of in shards:
        steps = jax.random.uniform(jax.random.fold_in(jax.random.fold_in(own_key, 6), dim), (shards_of,), jnp.float32, least / len(shards), high / len(shards))
        gain = gain * jnp.repeat(jnp.exp(steps), dims[dim] // shards_of).reshape((-1,) + (1,) * (len(dims) - 1 - dim))
    return gain


def bell_draw(own_key, shape, scale, limit, pieces=(), kind=jnp.bfloat16):
    values = jax.random.normal(own_key, shape, jnp.float32) * scale
    if len(pieces) > 0:
        values = levels(own_key, shape, pieces, -0.22, 0.18) * values
    return jnp.clip(values, min=-limit, max=limit).astype(kind)


def setup_inputs(seed: int = 0, part: int = 0) -> dict:
    seeds = jax.random.split(jax.random.key(seed), 10)
    part_splits = jax.random.split(jax.random.fold_in(seeds[9], part), 10)
    return {
        "cotangent": bell_draw(part_splits[0], (DPS, TOK_DEV, D), 1.0, 6.0, ((0, 4), (1, 4))),
        "gate_pre": bell_draw(part_splits[1], (TOKENS, FF), 1.5, 8.0, ((0, 4), (1, 4))),
        "up_pre": bell_draw(part_splits[2], (TOKENS, FF), 1.0, 6.0, ((0, 4), (1, 4))),
        "down_weight": bell_draw(seeds[3], (FF, D), FF ** -0.5, 0.0546875, ((0, 4),)),
        "adapter_in": bell_draw(part_splits[4], (ADAPTERS, RANK, FF), 0.03, 0.19921875, ((0, 4), (2, 4))),
        "adapter_out": bell_draw(part_splits[5], (ADAPTERS, RANK, D), D ** -0.5, 0.125, ((0, 4), (2, 4))),
        "token_adapter": draw_token_adapter(jax.random.fold_in(jax.random.fold_in(seeds[9], part), 71), part),
        "live_rows": draw_live_rows(jax.random.fold_in(jax.random.fold_in(seeds[9], part), 71), part),
        "adapter_slot": draw_adapter_slot(jax.random.fold_in(jax.random.fold_in(seeds[9], part), 71), part),
    }


lowrank_scale_factor = 2.0


def reference(cotangent, gate_pre, up_pre, down_weight, adapter_in, adapter_out, token_adapter, live_rows, adapter_slot):
    rows_flat = cotangent.reshape(TOKENS, D)
    position = jnp.arange(TOKENS, dtype=jnp.int32)
    live_token = jnp.repeat(live_rows, BLOCK, total_repeat_length=TOKENS)
    keep = (position % BLOCK) < live_token
    masked = jnp.where(keep[:, None], rows_flat, jnp.zeros((), jnp.bfloat16))
    gate_val = gate_pre.astype(jnp.float32)
    up_val = up_pre.astype(jnp.float32)
    sigma = jax.nn.sigmoid(gate_val)
    hidden = (gate_val * sigma * up_val).astype(jnp.bfloat16)
    block_ids = token_adapter.reshape(NBLK, BLOCK)[:, 0]
    slots = adapter_slot[block_ids].astype(jnp.int32)
    block_in = adapter_in[slots].astype(jnp.float32)
    block_out = adapter_out[slots].astype(jnp.float32)
    hidden_block_rows = hidden.reshape(NBLK, BLOCK, FF).astype(jnp.float32)
    masked_block_rows = masked.reshape(NBLK, BLOCK, D).astype(jnp.float32)
    lowrank_input = jnp.einsum("bnf,brf->bnr", hidden_block_rows, block_in).astype(jnp.bfloat16)
    lowrank_gradient = jnp.einsum("bnd,brd->bnr", masked_block_rows, block_out).astype(jnp.bfloat16)
    frozen_output = jnp.dot(masked, down_weight.T, preferred_element_type=jnp.float32)
    adapter_applied = jnp.einsum("bnr,brf->bnf", lowrank_gradient.astype(jnp.float32), block_in).reshape(TOKENS, FF)
    hidden_gradient = frozen_output + lowrank_scale_factor * adapter_applied
    gate_grad = (hidden_gradient * up_val * sigma * (1.0 + gate_val * (1.0 - sigma))).astype(jnp.bfloat16)
    up_grad = (hidden_gradient * gate_val * sigma).astype(jnp.bfloat16)
    incoming_terms = lowrank_scale_factor * jnp.einsum("oqx,oqg->oxg", lowrank_gradient.astype(jnp.float32), hidden_block_rows)
    outgoing_terms = lowrank_scale_factor * jnp.einsum("ykx,ykz->yxz", lowrank_input.astype(jnp.float32), masked_block_rows)
    grad_in = jnp.zeros((ADAPTERS, RANK, FF), jnp.float32).at[slots].add(incoming_terms).astype(jnp.bfloat16)
    grad_out = jnp.zeros((ADAPTERS, RANK, D), jnp.float32).at[slots].add(outgoing_terms).astype(jnp.bfloat16)
    return gate_grad, up_grad, grad_in, grad_out
```

```python
import functools

import jax
import jax.numpy as jnp
from jax import lax
from jax.experimental import pallas as pl
from jax.experimental.pallas import tpu as pltpu
from jax.sharding import PartitionSpec as P

BLOCK = 128
MESH = pl.DeviceIdType.MESH
NT = (((1,), (1,)), ((), ()))
TN = (((0,), (0,)), ((), ()))
VMEM_BYTES = 60 * 2**20
K_AIN, K_AOUT, K_GIN, K_GOUT, K_AO, K_LB, K_LI, K_TO = range(8)


lowrank_scale_factor = 2.0


def owned_sum(slot_ids, owner_index, owned, terms):
    local_ids = slot_ids % owned
    belongs = slot_ids // owned == owner_index
    selector = (local_ids[None, :] == jnp.arange(owned, dtype=jnp.int32)[:, None]) & belongs[
        None, :
    ]
    flat = terms.reshape(terms.shape[0], -1)
    summed = jnp.dot(
        selector.astype(jnp.float32),
        flat,
        precision=lax.Precision.HIGHEST,
        preferred_element_type=jnp.float32,
    )
    return summed.reshape((owned,) + terms.shape[1:])


def local(
    cotangent,
    gate_pre,
    up_pre,
    down_weight,
    adapter_in,
    adapter_out,
    token_adapter,
    live_rows,
    adapter_slot,
):
    dp_count = lax.axis_size("dp")
    dp_index = lax.axis_index("dp")
    tensor_index = lax.axis_index("tensor")
    tok_rows, ff_local = gate_pre.shape
    width = cotangent.shape[2]
    feat_local = adapter_out.shape[2]
    owned = adapter_in.shape[0]
    blocks = tok_rows // BLOCK
    total_blocks = live_rows.shape[0]
    gathered = lax.all_gather(cotangent, "tensor", axis=1, tiled=True)[0]
    block_ids = token_adapter.reshape(total_blocks, BLOCK)[:, 0]
    adapter_count = adapter_slot.shape[0]
    lookup = block_ids[:, None] == jnp.arange(adapter_count, dtype=jnp.int32)[None, :]
    all_slots = jnp.sum(jnp.where(lookup, adapter_slot[None, :], 0), axis=1)
    my_slots = lax.dynamic_slice_in_dim(all_slots, dp_index * blocks, blocks)
    my_live = lax.dynamic_slice_in_dim(live_rows, dp_index * blocks, blocks)
    slot_grid = all_slots.reshape(dp_count, blocks)
    owner_grid = slot_grid // owned
    my_owner = lax.dynamic_index_in_dim(owner_grid, dp_index, 0, keepdims=False)
    keep = jnp.arange(BLOCK, dtype=jnp.int32)[None, :] < my_live[:, None]
    masked = jnp.where(keep.reshape(tok_rows, 1), gathered, jnp.zeros((), jnp.bfloat16))
    gate_val = gate_pre.astype(jnp.float32)
    up_val = up_pre.astype(jnp.float32)
    sigma = jax.nn.sigmoid(gate_val)
    hidden = (gate_val * sigma * up_val).astype(jnp.bfloat16)
    every_in, every_out = (
        lax.all_gather(adapter_in, "dp", axis=0, tiled=True),
        lax.all_gather(adapter_out, "dp", axis=0, tiled=True),
    )
    block_in = every_in[my_slots]
    block_out = every_out[my_slots]
    hidden_block_rows = hidden.reshape(blocks, BLOCK, ff_local)
    masked_block_rows = masked.reshape(blocks, BLOCK, width)
    masked_local = lax.dynamic_slice_in_dim(
        masked_block_rows, tensor_index * feat_local, feat_local, 2
    )
    part_in = jnp.einsum(
        "bnf,brf->bnr", hidden_block_rows, block_in, preferred_element_type=jnp.float32
    )
    part_back = jnp.einsum(
        "bnd,brd->bnr", masked_local, block_out, preferred_element_type=jnp.float32
    )
    lowrank_input, lowrank_gradient = lax.psum((part_in, part_back), "tensor")
    lowrank_input = lowrank_input.astype(jnp.bfloat16)
    lowrank_gradient = lowrank_gradient.astype(jnp.bfloat16)
    frozen_output = lax.dot_general(
        masked, down_weight, (((1,), (1,)), ((), ())), preferred_element_type=jnp.float32
    )
    adapter_applied = jnp.einsum(
        "bnr,brf->bnf", lowrank_gradient, block_in, preferred_element_type=jnp.float32
    ).reshape(tok_rows, ff_local)
    hidden_gradient = frozen_output + lowrank_scale_factor * adapter_applied
    gate_grad = (hidden_gradient * up_val * sigma * (1.0 + gate_val * (1.0 - sigma))).astype(
        jnp.bfloat16
    )
    up_grad = (hidden_gradient * gate_val * sigma).astype(jnp.bfloat16)
    incoming_terms = lowrank_scale_factor * jnp.einsum(
        "oqx,oqg->oxg", lowrank_gradient, hidden_block_rows, preferred_element_type=jnp.float32
    )
    outgoing_terms = lowrank_scale_factor * jnp.einsum(
        "ykx,ykz->yxz", lowrank_input, masked_local, preferred_element_type=jnp.float32
    )
    route = my_owner[None, :] == jnp.arange(dp_count, dtype=jnp.int32)[:, None]
    send_terms_in = jnp.where(route[:, :, None, None], incoming_terms[None], 0.0)
    send_terms_out = jnp.where(route[:, :, None, None], outgoing_terms[None], 0.0)
    got_terms_in, got_terms_out = (
        lax.all_to_all(send_terms_in, "dp", split_axis=0, concat_axis=0, tiled=True),
        lax.all_to_all(send_terms_out, "dp", split_axis=0, concat_axis=0, tiled=True),
    )
    grad_in = owned_sum(
        all_slots,
        dp_index,
        owned,
        got_terms_in.reshape((dp_count * blocks,) + incoming_terms.shape[1:]),
    )
    grad_out = owned_sum(
        all_slots,
        dp_index,
        owned,
        got_terms_out.reshape((dp_count * blocks,) + outgoing_terms.shape[1:]),
    )
    return (gate_grad, up_grad, grad_in.astype(jnp.bfloat16), grad_out.astype(jnp.bfloat16))


def dotf(a, b, dims=(((1,), (0,)), ((), ()))):
    return lax.dot_general(a, b, dims, preferred_element_type=jnp.float32)


def fused_kernel(
    n,
    m,
    chunks,
    tile,
    ids,
    live,
    slot_of,
    cot,
    gate,
    up,
    weight,
    ain,
    aout,
    out_g,
    out_u,
    out_gi,
    out_go,
    cotv,
    mg,
    gv,
    uv,
    wv,
    hid,
    fa,
    fb,
    acc,
    aiv,
    aov,
    s_in,
    s_out,
    r_in,
    r_out,
    bi,
    s_ao,
    r_ao,
    r_lb,
    s_li,
    r_li,
    s_to,
    r_to,
    s_gi,
    s_go,
    gsend,
    grecv,
    ssend,
    srecv,
    lsem,
    osem,
):
    z = lax.axis_index("tensor")
    d = lax.axis_index("dp")
    width = cot.shape[1]
    feat = aov.shape[2]
    ff = gate.shape[1]
    owned = aov.shape[0]
    blocks = gv.shape[0]
    kc = width // chunks
    ftiles = ff // tile

    loads = [
        pltpu.make_async_copy(cot, cotv, lsem.at[0]),
        pltpu.make_async_copy(aout, aov, lsem.at[1]),
        pltpu.make_async_copy(ain, aiv, lsem.at[2]),
    ]
    gu = []
    for b in range(blocks):
        rows = pl.ds(b * BLOCK, BLOCK)
        gu.append(
            (
                pltpu.make_async_copy(gate.at[rows], gv.at[b], lsem.at[4 + 2 * b]),
                pltpu.make_async_copy(up.at[rows], uv.at[b], lsem.at[5 + 2 * b]),
            )
        )
    wload = pltpu.make_async_copy(weight, wv, lsem.at[3])
    for c in loads:
        c.start()
    for pair in gu:
        pair[0].start()
        pair[1].start()
    wload.start()

    def slot(block):
        return slot_of[ids[block * BLOCK]]

    def my_slot(b):
        return slot(d * blocks + b)

    barrier = pltpu.get_barrier_semaphore()
    for k in range(1, n):
        pl.semaphore_signal(
            barrier, inc=1, device_id={"tensor": lax.rem(z + k, n)}, device_id_type=MESH
        )
    for k in range(1, m):
        pl.semaphore_signal(
            barrier, inc=1, device_id={"dp": lax.rem(d + k, m)}, device_id_type=MESH
        )
    pl.semaphore_wait(barrier, n - 1 + m - 1)

    def piece(direction, shard, c):
        part = mg.at[shard, :, pl.ds(c * kc, kc)]
        return pltpu.make_async_remote_copy(
            src_ref=part,
            dst_ref=part,
            send_sem=gsend.at[direction, shard, c],
            recv_sem=grecv.at[shard, c],
            device_id={"tensor": z - 1 if direction == 0 else z + 1},
            device_id_type=MESH,
        )

    def small(kind, src, dst, k, axis):
        me, size = (z, n) if axis == "tensor" else (d, m)
        peer = lax.rem(me + k, size)
        return pltpu.make_async_remote_copy(
            src_ref=src.at[peer] if src is not dst else src.at[me],
            dst_ref=dst.at[me],
            send_sem=ssend.at[kind, peer],
            recv_sem=srecv.at[kind, me],
            device_id={axis: peer},
            device_id_type=MESH,
        )

    def arrived(kind, src, dst, k, axis):
        me, size = (z, n) if axis == "tensor" else (d, m)
        frm = lax.rem(me + k, size)
        pltpu.make_async_remote_copy(
            src_ref=src.at[frm],
            dst_ref=dst.at[frm],
            send_sem=ssend.at[kind, frm],
            recv_sem=srecv.at[kind, frm],
            device_id={axis: frm},
            device_id_type=MESH,
        ).wait_recv()

    loads[0].wait()
    count = live[d * blocks + z]
    keep = lax.broadcasted_iota(jnp.int32, (BLOCK, kc), 0) < count
    for c in range(chunks):
        cols = pl.ds(c * kc, kc)
        val = cotv[:, cols].astype(jnp.float32)
        mg[z, :, cols] = jnp.where(keep, val, 0.0).astype(jnp.bfloat16)
        for direction in range(2):

            @pl.when(z > 0 if direction == 0 else z < n - 1)
            def _():
                piece(direction, z, c).start()

    loads[1].wait()
    loads[2].wait()
    for e in range(m):
        index = jnp.int32(0)
        for b in range(blocks):
            s = slot(e * blocks + b)
            index = jnp.where(s // owned == d, s % owned, index)
        s_out[e] = aov[index]
        s_in[e] = aiv[index]
    for k in range(1, m):
        small(K_AOUT, s_out, r_out, k, "dp").start()
    for k in range(1, m):
        small(K_AIN, s_in, r_in, k, "dp").start()
    r_out[d] = s_out[d]
    r_in[d] = s_in[d]

    for b in range(blocks):
        gu[b][0].wait()
        gu[b][1].wait()

        def row_group(i, carry, b=b):
            rows = pl.ds(pl.multiple_of(i * 16, 16), 16)
            for j in range(ftiles):
                cols = pl.ds(j * tile, tile)
                g = gv[b, rows, cols].astype(jnp.float32)
                u = uv[b, rows, cols].astype(jnp.float32)
                s = jax.nn.sigmoid(g)
                gs = g * s
                hid[b, rows, cols] = (gs * u).astype(jnp.bfloat16)
                fb[b, rows, cols] = gs
                fa[b, rows, cols] = u * s * (1.0 + g * (1.0 - s))
            return carry

        lax.fori_loop(0, BLOCK // 16, row_group, 0)

    for k in range(1, m):
        arrived(K_AOUT, s_out, r_out, k, "dp")
    for b in range(n):
        s_ao[b] = r_out[my_slot(b) // owned]
    r_ao[z] = s_ao[z]
    for k in range(1, n):
        small(K_AO, s_ao, r_ao, k, "tensor").start()

    for k in range(1, m):
        arrived(K_AIN, s_in, r_in, k, "dp")
    for b in range(blocks):
        bi[b] = r_in[my_slot(b) // owned]
        s_li[b] = dotf(bi[b], hid[b], NT)
    r_li[z] = s_li[z]
    for k in range(1, n):
        small(K_LI, s_li, r_li, k, "tensor").start()

    for k in range(1, n):
        arrived(K_AO, s_ao, r_ao, k, "tensor")
    back = jnp.zeros((r_lb.shape[1], BLOCK), jnp.float32)
    for q in range(n):
        back = back + dotf(r_ao[q], mg[z, :, pl.ds(q * feat, feat)], NT)
    r_lb[z] = back.astype(jnp.bfloat16)
    for k in range(1, n):
        small(K_LB, r_lb, r_lb, k, "tensor").start()

    def poll(step, c):
        @pl.when(z + step < n)
        def _():
            piece(0, z + step, c).wait_recv()

            @pl.when(z > 0)
            def _():
                piece(0, z + step, c).start()

        @pl.when(z - step >= 0)
        def _():
            piece(1, z - step, c).wait_recv()

            @pl.when(z < n - 1)
            def _():
                piece(1, z - step, c).start()

    def outputs(b):
        rows = pl.ds(pl.multiple_of(b * BLOCK, BLOCK), BLOCK)
        return (
            pltpu.make_async_copy(gv.at[b], out_g.at[rows], osem.at[0, b]),
            pltpu.make_async_copy(uv.at[b], out_u.at[rows], osem.at[1, b]),
        )

    def accumulate(b, first, last, low, k0, size):
        def body(j, carry):
            cols = pl.ds(pl.multiple_of(j * tile, tile), tile)
            part = dotf(mg[b, :, pl.ds(k0, size)], wv[cols, pl.ds(k0, size)], NT)
            if not first:
                part = part + acc[b, :, cols]
            if low:
                part = part + 2.0 * dotf(r_lb[b], bi[b, :, cols], TN)
            if last:
                gv[b, :, cols] = (part * fa[b, :, cols]).astype(jnp.bfloat16)
                uv[b, :, cols] = (part * fb[b, :, cols]).astype(jnp.bfloat16)
            else:
                acc[b, :, cols] = part
            return carry

        lax.fori_loop(0, ftiles, body, 0)
        if last:
            for c in outputs(b):
                c.start()

    poll(1, 0)
    wload.wait()
    accumulate(z, True, True, True, 0, width)

    for k in range(1, n):
        arrived(K_LI, s_li, r_li, k, "tensor")
    low_in = r_li[0]
    for q in range(1, n):
        low_in = low_in + r_li[q]
    low_in = low_in.astype(jnp.bfloat16)
    for q in range(n):
        s_to[q] = (2.0 * dotf(low_in, mg[z, :, pl.ds(q * feat, feat)])).astype(jnp.bfloat16)
    r_to[z] = s_to[z]
    for k in range(1, n):
        small(K_TO, s_to, r_to, k, "tensor").start()

    for step in range(1, n):
        for c in range(chunks):
            if (step, c) != (1, 0):
                poll(step, c)
            low = c == (chunks - 1 if step == 1 else 0)
            if step == 1 and low:
                for k in range(1, n):
                    arrived(K_LB, r_lb, r_lb, k, "tensor")

            def side(i, carry, step=step, c=c, low=low):
                b = z + step - i * 2 * step

                @pl.when((b >= 0) & (b < n))
                def _():
                    accumulate(b, c == 0, c == chunks - 1, low, c * kc, kc)

                return carry

            lax.fori_loop(0, 2, side, 0)
            if step == 1 and low:
                for k in range(1, n):
                    arrived(K_TO, s_to, r_to, k, "tensor")
                for o in range(m):
                    index = jnp.int32(0)
                    valid = jnp.float32(0.0)
                    for b in range(blocks):
                        hit = my_slot(b) // owned == o
                        index = jnp.where(hit, b, index)
                        valid = jnp.where(hit, 1.0, valid)
                    s_go[o] = (r_to[index].astype(jnp.float32) * valid).astype(jnp.bfloat16)
                    lb = r_lb[index]

                    def term(j, carry, o=o, lb=lb, index=index, valid=valid):
                        cols = pl.ds(pl.multiple_of(j * tile, tile), tile)
                        s_gi[o, :, cols] = (
                            (2.0 * valid) * dotf(lb, hid[index, :, cols])
                        ).astype(jnp.bfloat16)
                        return carry

                    lax.fori_loop(0, ftiles, term, 0)
                for k in range(1, m):
                    small(K_GIN, s_gi, out_gi, k, "dp").start()
                    small(K_GOUT, s_go, out_go, k, "dp").start()
                own = (
                    pltpu.make_async_copy(s_gi.at[d], out_gi.at[d], lsem.at[0]),
                    pltpu.make_async_copy(s_go.at[d], out_go.at[d], lsem.at[1]),
                )
                for cp in own:
                    cp.start()

    for cp in own:
        cp.wait()
    for k in range(1, m):
        arrived(K_GIN, s_gi, out_gi, k, "dp")
        arrived(K_GOUT, s_go, out_go, k, "dp")
    for k in range(1, m):
        small(K_AIN, s_in, r_in, k, "dp").wait_send()
        small(K_AOUT, s_out, r_out, k, "dp").wait_send()
        small(K_GIN, s_gi, out_gi, k, "dp").wait_send()
        small(K_GOUT, s_go, out_go, k, "dp").wait_send()
    for k in range(1, n):
        small(K_AO, s_ao, r_ao, k, "tensor").wait_send()
        small(K_LB, r_lb, r_lb, k, "tensor").wait_send()
        small(K_LI, s_li, r_li, k, "tensor").wait_send()
        small(K_TO, s_to, r_to, k, "tensor").wait_send()
    for shard in range(n):
        for c in range(chunks):

            @pl.when((z > 0) & (shard >= z))
            def _():
                piece(0, shard, c).wait_send()

            @pl.when((z < n - 1) & (shard <= z))
            def _():
                piece(1, shard, c).wait_send()

    for b in range(n):
        for cp in outputs(b):
            cp.wait()


def finish_kernel(m, ids, slot_of, g, u, gi, go, out_g, out_u, out_gi, out_go, vi, vo, zi, zo, sem):
    d = lax.axis_index("dp")
    owned = out_gi.shape[0]
    blocks = g.shape[0] // BLOCK
    copies = []
    for b in range(blocks):
        rows = pl.ds(b * BLOCK, BLOCK)
        copies.append(pltpu.make_async_copy(g.at[rows], out_g.at[rows], sem.at[2 * b]))
        copies.append(pltpu.make_async_copy(u.at[rows], out_u.at[rows], sem.at[2 * b + 1]))
    for cp in copies:
        cp.start()
    loads = (
        pltpu.make_async_copy(gi, vi, sem.at[2 * blocks]),
        pltpu.make_async_copy(go, vo, sem.at[2 * blocks + 1]),
    )
    for cp in loads:
        cp.start()

    def clear(s, carry):
        zi[s] = jnp.zeros(zi.shape[1:], zi.dtype)
        zo[s] = jnp.zeros(zo.shape[1:], zo.dtype)
        return carry

    lax.fori_loop(0, owned, clear, 0)
    picks = []
    for e in range(m):
        index = jnp.int32(0)
        hits = jnp.int32(0)
        for b in range(blocks):
            s = slot_of[ids[(e * blocks + b) * BLOCK]]
            hit = s // owned == d
            index = jnp.where(hit, s % owned, index)
            hits = jnp.where(hit, 1, hits)
        picks.append((index, hits > 0))
    for cp in loads:
        cp.wait()
    for e in range(m):

        @pl.when(picks[e][1])
        def _():
            for src, dst in ((vi, zi), (vo, zo)):
                total = jnp.zeros(src.shape[1:], jnp.float32)
                for f in range(m):
                    same = picks[f][1] & (picks[f][0] == picks[e][0])
                    total = total + jnp.where(same, src[f].astype(jnp.float32), 0.0)
                dst[picks[e][0]] = total.astype(dst.dtype)

    stores = (
        pltpu.make_async_copy(zi, out_gi, sem.at[2 * blocks + 2]),
        pltpu.make_async_copy(zo, out_go, sem.at[2 * blocks + 3]),
    )
    for cp in stores:
        cp.start()
    for cp in stores:
        cp.wait()
    for cp in copies:
        cp.wait()


def fused(
    n,
    m,
    chunks,
    cotangent,
    gate_pre,
    up_pre,
    down_weight,
    adapter_in,
    adapter_out,
    token_adapter,
    live_rows,
    adapter_slot,
):
    tok, ff = gate_pre.shape
    blocks = tok // BLOCK
    cot = cotangent[0]
    width = cot.shape[1]
    owned, rank, feat = adapter_out.shape
    tile = next(t for t in (640, 512, 256, 128) if ff % t == 0)
    bf, f32 = jnp.bfloat16, jnp.float32
    anyspec = pl.BlockSpec(memory_space=pl.ANY)
    smem = pl.BlockSpec(memory_space=pltpu.SMEM)
    big = max(n, m)
    g, u, gi, go = pl.pallas_call(
        functools.partial(fused_kernel, n, m, chunks, tile),
        out_shape=(
            jax.ShapeDtypeStruct((tok, ff), bf),
            jax.ShapeDtypeStruct((tok, ff), bf),
            jax.ShapeDtypeStruct((m, rank, ff), bf),
            jax.ShapeDtypeStruct((m, rank, feat), bf),
        ),
        in_specs=[smem] * 3 + [anyspec] * 6,
        out_specs=(anyspec,) * 4,
        scratch_shapes=[
            pltpu.VMEM((BLOCK, width), bf),
            pltpu.VMEM((n, BLOCK, width), bf),
            pltpu.VMEM((blocks, BLOCK, ff), bf),
            pltpu.VMEM((blocks, BLOCK, ff), bf),
            pltpu.VMEM(down_weight.shape, bf),
            pltpu.VMEM((blocks, BLOCK, ff), bf),
            pltpu.VMEM((blocks, BLOCK, ff), f32),
            pltpu.VMEM((blocks, BLOCK, ff), f32),
            pltpu.VMEM((blocks, BLOCK, ff), f32),
            pltpu.VMEM(adapter_in.shape, bf),
            pltpu.VMEM(adapter_out.shape, bf),
            pltpu.VMEM((m, rank, ff), bf),
            pltpu.VMEM((m, rank, feat), bf),
            pltpu.VMEM((m, rank, ff), bf),
            pltpu.VMEM((m, rank, feat), bf),
            pltpu.VMEM((blocks, rank, ff), bf),
            pltpu.VMEM((n, rank, feat), bf),
            pltpu.VMEM((n, rank, feat), bf),
            pltpu.VMEM((n, rank, BLOCK), bf),
            pltpu.VMEM((n, rank, BLOCK), f32),
            pltpu.VMEM((n, rank, BLOCK), f32),
            pltpu.VMEM((n, rank, feat), bf),
            pltpu.VMEM((n, rank, feat), bf),
            pltpu.VMEM((m, rank, ff), bf),
            pltpu.VMEM((m, rank, feat), bf),
            pltpu.SemaphoreType.DMA((2, n, chunks)),
            pltpu.SemaphoreType.DMA((n, chunks)),
            pltpu.SemaphoreType.DMA((8, big)),
            pltpu.SemaphoreType.DMA((8, big)),
            pltpu.SemaphoreType.DMA((4 + 2 * blocks,)),
            pltpu.SemaphoreType.DMA((2, blocks)),
        ],
        compiler_params=pltpu.CompilerParams(
            collective_id=0, has_side_effects=True, vmem_limit_bytes=VMEM_BYTES
        ),
        name="fused_backward",
    )(
        token_adapter,
        live_rows,
        adapter_slot,
        cot,
        gate_pre,
        up_pre,
        down_weight,
        adapter_in,
        adapter_out,
    )
    return pl.pallas_call(
        functools.partial(finish_kernel, m),
        out_shape=(
            jax.ShapeDtypeStruct((tok, ff), bf),
            jax.ShapeDtypeStruct((tok, ff), bf),
            jax.ShapeDtypeStruct(adapter_in.shape, bf),
            jax.ShapeDtypeStruct(adapter_out.shape, bf),
        ),
        in_specs=[smem] * 2 + [anyspec] * 4,
        out_specs=(anyspec,) * 4,
        scratch_shapes=[
            pltpu.VMEM((m, rank, ff), bf),
            pltpu.VMEM((m, rank, feat), bf),
            pltpu.VMEM(adapter_in.shape, bf),
            pltpu.VMEM(adapter_out.shape, bf),
            pltpu.SemaphoreType.DMA((2 * blocks + 4,)),
        ],
        compiler_params=pltpu.CompilerParams(vmem_limit_bytes=32 * 2**20),
        name="finish",
    )(token_adapter, adapter_slot, g, u, gi, go)


CHUNKS = 2


def dispatch(*args):
    cotangent, gate_pre, _, _, _, adapter_out = args[:6]
    n, m = lax.axis_size("tensor"), lax.axis_size("dp")
    tok, ff = gate_pre.shape
    aligned = (
        cotangent.shape[1] == BLOCK
        and tok == n * BLOCK
        and ff % 128 == 0
        and adapter_out.shape[2] % 128 == 0
        and cotangent.shape[2] % (128 * CHUNKS) == 0
    )
    if aligned:
        return fused(n, m, CHUNKS, *args)
    return local(*args)


def solution(mesh):
    placed = (
        P("dp", ("groups", "tensor"), None),
        P(("groups", "dp"), "tensor"),
        P(("groups", "dp"), "tensor"),
        P("tensor", None),
        P(("groups", "dp"), None, "tensor"),
        P(("groups", "dp"), None, "tensor"),
        P("groups"),
        P("groups"),
        P("groups"),
    )
    return jax.shard_map(
        dispatch,
        mesh=mesh,
        in_specs=placed,
        out_specs=(
            P(("groups", "dp"), "tensor"),
            P(("groups", "dp"), "tensor"),
            P(("groups", "dp"), None, "tensor"),
            P(("groups", "dp"), None, "tensor"),
        ),
        check_vma=False,
    )
```

```python
import functools

import jax
import jax.numpy as jnp
from jax import lax
from jax.experimental import pallas as pl
from jax.experimental.pallas import tpu as pltpu
from jax.sharding import PartitionSpec as P

BLOCK = 128
MESH = pl.DeviceIdType.MESH
NT = (((1,), (1,)), ((), ()))
TN = (((0,), (0,)), ((), ()))
VMEM_BYTES = 50 * 2**20
K_AIN, K_AOUT, K_GIN, K_GOUT, K_AO, K_LB, K_LI, K_TO = range(8)


lowrank_scale_factor = 2.0


def owned_sum(slot_ids, owner_index, owned, terms):
    local_ids = slot_ids % owned
    belongs = slot_ids // owned == owner_index
    selector = (local_ids[None, :] == jnp.arange(owned, dtype=jnp.int32)[:, None]) & belongs[
        None, :
    ]
    flat = terms.reshape(terms.shape[0], -1)
    summed = jnp.dot(
        selector.astype(jnp.float32),
        flat,
        precision=lax.Precision.HIGHEST,
        preferred_element_type=jnp.float32,
    )
    return summed.reshape((owned,) + terms.shape[1:])


def local(
    cotangent,
    gate_pre,
    up_pre,
    down_weight,
    adapter_in,
    adapter_out,
    token_adapter,
    live_rows,
    adapter_slot,
):
    dp_count = lax.axis_size("dp")
    dp_index = lax.axis_index("dp")
    tensor_index = lax.axis_index("tensor")
    tok_rows, ff_local = gate_pre.shape
    width = cotangent.shape[2]
    feat_local = adapter_out.shape[2]
    owned = adapter_in.shape[0]
    blocks = tok_rows // BLOCK
    total_blocks = live_rows.shape[0]
    gathered = lax.all_gather(cotangent, "tensor", axis=1, tiled=True)[0]
    block_ids = token_adapter.reshape(total_blocks, BLOCK)[:, 0]
    adapter_count = adapter_slot.shape[0]
    lookup = block_ids[:, None] == jnp.arange(adapter_count, dtype=jnp.int32)[None, :]
    all_slots = jnp.sum(jnp.where(lookup, adapter_slot[None, :], 0), axis=1)
    my_slots = lax.dynamic_slice_in_dim(all_slots, dp_index * blocks, blocks)
    my_live = lax.dynamic_slice_in_dim(live_rows, dp_index * blocks, blocks)
    slot_grid = all_slots.reshape(dp_count, blocks)
    owner_grid = slot_grid // owned
    my_owner = lax.dynamic_index_in_dim(owner_grid, dp_index, 0, keepdims=False)
    keep = jnp.arange(BLOCK, dtype=jnp.int32)[None, :] < my_live[:, None]
    masked = jnp.where(keep.reshape(tok_rows, 1), gathered, jnp.zeros((), jnp.bfloat16))
    gate_val = gate_pre.astype(jnp.float32)
    up_val = up_pre.astype(jnp.float32)
    sigma = jax.nn.sigmoid(gate_val)
    hidden = (gate_val * sigma * up_val).astype(jnp.bfloat16)
    every_in, every_out = (
        lax.all_gather(adapter_in, "dp", axis=0, tiled=True),
        lax.all_gather(adapter_out, "dp", axis=0, tiled=True),
    )
    block_in = every_in[my_slots]
    block_out = every_out[my_slots]
    hidden_block_rows = hidden.reshape(blocks, BLOCK, ff_local)
    masked_block_rows = masked.reshape(blocks, BLOCK, width)
    masked_local = lax.dynamic_slice_in_dim(
        masked_block_rows, tensor_index * feat_local, feat_local, 2
    )
    part_in = jnp.einsum(
        "bnf,brf->bnr", hidden_block_rows, block_in, preferred_element_type=jnp.float32
    )
    part_back = jnp.einsum(
        "bnd,brd->bnr", masked_local, block_out, preferred_element_type=jnp.float32
    )
    lowrank_input, lowrank_gradient = lax.psum((part_in, part_back), "tensor")
    lowrank_input = lowrank_input.astype(jnp.bfloat16)
    lowrank_gradient = lowrank_gradient.astype(jnp.bfloat16)
    frozen_output = lax.dot_general(
        masked, down_weight, (((1,), (1,)), ((), ())), preferred_element_type=jnp.float32
    )
    adapter_applied = jnp.einsum(
        "bnr,brf->bnf", lowrank_gradient, block_in, preferred_element_type=jnp.float32
    ).reshape(tok_rows, ff_local)
    hidden_gradient = frozen_output + lowrank_scale_factor * adapter_applied
    gate_grad = (hidden_gradient * up_val * sigma * (1.0 + gate_val * (1.0 - sigma))).astype(
        jnp.bfloat16
    )
    up_grad = (hidden_gradient * gate_val * sigma).astype(jnp.bfloat16)
    incoming_terms = lowrank_scale_factor * jnp.einsum(
        "oqx,oqg->oxg", lowrank_gradient, hidden_block_rows, preferred_element_type=jnp.float32
    )
    outgoing_terms = lowrank_scale_factor * jnp.einsum(
        "ykx,ykz->yxz", lowrank_input, masked_local, preferred_element_type=jnp.float32
    )
    route = my_owner[None, :] == jnp.arange(dp_count, dtype=jnp.int32)[:, None]
    send_terms_in = jnp.where(route[:, :, None, None], incoming_terms[None], 0.0)
    send_terms_out = jnp.where(route[:, :, None, None], outgoing_terms[None], 0.0)
    got_terms_in, got_terms_out = (
        lax.all_to_all(send_terms_in, "dp", split_axis=0, concat_axis=0, tiled=True),
        lax.all_to_all(send_terms_out, "dp", split_axis=0, concat_axis=0, tiled=True),
    )
    grad_in = owned_sum(
        all_slots,
        dp_index,
        owned,
        got_terms_in.reshape((dp_count * blocks,) + incoming_terms.shape[1:]),
    )
    grad_out = owned_sum(
        all_slots,
        dp_index,
        owned,
        got_terms_out.reshape((dp_count * blocks,) + outgoing_terms.shape[1:]),
    )
    return (gate_grad, up_grad, grad_in.astype(jnp.bfloat16), grad_out.astype(jnp.bfloat16))


def dotf(a, b, dims=(((1,), (0,)), ((), ()))):
    return lax.dot_general(a, b, dims, preferred_element_type=jnp.float32)


def fused_kernel(
    n,
    m,
    chunk_sizes,
    tile,
    ids,
    live,
    slot_of,
    cot,
    gate,
    up,
    weight,
    ain,
    aout,
    gv,
    uv,
    out_gi,
    out_go,
    cotv,
    mg,
    wv,
    hid,
    fa,
    fb,
    acc,
    aiv,
    aov,
    s_in,
    s_out,
    r_in,
    r_out,
    bi,
    s_ao,
    r_ao,
    r_lb,
    s_li,
    r_li,
    s_to,
    r_to,
    s_gi,
    s_go,
    gsend,
    grecv,
    ssend,
    srecv,
    lsem,
):
    z = lax.axis_index("tensor")
    d = lax.axis_index("dp")
    width = cot.shape[1]
    feat = aov.shape[2]
    ff = gate.shape[1]
    owned = aov.shape[0]
    blocks = gv.shape[0]
    sizes = chunk_sizes
    starts = [sum(sizes[:i]) for i in range(len(sizes))]
    chunks = len(sizes)
    ftiles = ff // tile

    loads = [
        pltpu.make_async_copy(cot, cotv, lsem.at[0]),
        pltpu.make_async_copy(aout, aov, lsem.at[1]),
        pltpu.make_async_copy(ain, aiv, lsem.at[2]),
    ]
    gu = []
    for b in range(blocks):
        rows = pl.ds(b * BLOCK, BLOCK)
        gu.append(
            (
                pltpu.make_async_copy(gate.at[rows], gv.at[b], lsem.at[4 + 2 * b]),
                pltpu.make_async_copy(up.at[rows], uv.at[b], lsem.at[5 + 2 * b]),
            )
        )
    wload = pltpu.make_async_copy(weight, wv, lsem.at[3])
    for c in loads:
        c.start()

    def slot(block):
        return slot_of[ids[block * BLOCK]]

    def my_slot(b):
        return slot(d * blocks + b)

    barrier = pltpu.get_barrier_semaphore()
    for k in range(1, n):
        pl.semaphore_signal(
            barrier, inc=1, device_id={"tensor": lax.rem(z + k, n)}, device_id_type=MESH
        )
    for k in range(1, m):
        pl.semaphore_signal(
            barrier, inc=1, device_id={"dp": lax.rem(d + k, m)}, device_id_type=MESH
        )
    pl.semaphore_wait(barrier, n - 1 + m - 1)

    def piece(direction, shard, c):
        part = mg.at[shard, :, pl.ds(starts[c], sizes[c])]
        return pltpu.make_async_remote_copy(
            src_ref=part,
            dst_ref=part,
            send_sem=gsend.at[direction, shard, c],
            recv_sem=grecv.at[shard, c],
            device_id={"tensor": z - 1 if direction == 0 else z + 1},
            device_id_type=MESH,
        )

    def small(kind, src, dst, k, axis):
        me, size = (z, n) if axis == "tensor" else (d, m)
        peer = lax.rem(me + k, size)
        return pltpu.make_async_remote_copy(
            src_ref=src.at[peer] if src is not dst else src.at[me],
            dst_ref=dst.at[me],
            send_sem=ssend.at[kind, peer],
            recv_sem=srecv.at[kind, me],
            device_id={axis: peer},
            device_id_type=MESH,
        )

    def arrived(kind, src, dst, k, axis):
        me, size = (z, n) if axis == "tensor" else (d, m)
        frm = lax.rem(me + k, size)
        pltpu.make_async_remote_copy(
            src_ref=src.at[frm],
            dst_ref=dst.at[frm],
            send_sem=ssend.at[kind, frm],
            recv_sem=srecv.at[kind, frm],
            device_id={axis: frm},
            device_id_type=MESH,
        ).wait_recv()

    loads[0].wait()
    count = live[d * blocks + z]
    for c in range(chunks):
        cols = pl.ds(starts[c], sizes[c])
        keep = lax.broadcasted_iota(jnp.int32, (BLOCK, sizes[c]), 0) < count
        val = cotv[:, cols].astype(jnp.float32)
        mg[z, :, cols] = jnp.where(keep, val, 0.0).astype(jnp.bfloat16)
        for direction in range(2):

            @pl.when(z > 0 if direction == 0 else z < n - 1)
            def _():
                piece(direction, z, c).start()

    for pair in gu:
        pair[0].start()
        pair[1].start()
    wload.start()

    loads[1].wait()
    loads[2].wait()
    for e in range(m):
        index = jnp.int32(0)
        for b in range(blocks):
            s = slot(e * blocks + b)
            index = jnp.where(s // owned == d, s % owned, index)
        s_out[e] = aov[index]
        s_in[e] = aiv[index]
    for k in range(1, m):
        small(K_AOUT, s_out, r_out, k, "dp").start()
    for k in range(1, m):
        small(K_AIN, s_in, r_in, k, "dp").start()
    r_out[d] = s_out[d]
    r_in[d] = s_in[d]

    for b in range(blocks):
        gu[b][0].wait()
        gu[b][1].wait()

        def row_group(i, carry, b=b):
            rows = pl.ds(pl.multiple_of(i * 16, 16), 16)
            for j in range(ftiles):
                cols = pl.ds(j * tile, tile)
                g = gv[b, rows, cols].astype(jnp.float32)
                u = uv[b, rows, cols].astype(jnp.float32)
                s = jax.nn.sigmoid(g)
                gs = g * s
                hid[b, rows, cols] = (gs * u).astype(jnp.bfloat16)
                fb[b, rows, cols] = gs
                fa[b, rows, cols] = u * s * (1.0 + g * (1.0 - s))
            return carry

        lax.fori_loop(0, BLOCK // 16, row_group, 0)

    for k in range(1, m):
        arrived(K_AIN, s_in, r_in, k, "dp")
    for b in range(blocks):
        bi[b] = r_in[my_slot(b) // owned]
        s_li[b] = dotf(bi[b], hid[b], NT)
    r_li[z] = s_li[z]
    for k in range(1, n):
        small(K_LI, s_li, r_li, k, "tensor").start()

    for k in range(1, m):
        arrived(K_AOUT, s_out, r_out, k, "dp")
    for b in range(n):
        s_ao[b] = r_out[my_slot(b) // owned]
    r_ao[z] = s_ao[z]
    for k in range(1, n):
        small(K_AO, s_ao, r_ao, k, "tensor").start()

    def poll(step, c):
        @pl.when(z + step < n)
        def _():
            piece(0, z + step, c).wait_recv()

            @pl.when(z > 0)
            def _():
                piece(0, z + step, c).start()

        @pl.when(z - step >= 0)
        def _():
            piece(1, z - step, c).wait_recv()

            @pl.when(z < n - 1)
            def _():
                piece(1, z - step, c).start()

    def accumulate(b, first, last, low, k0, size):
        def body(j, carry):
            cols = pl.ds(pl.multiple_of(j * tile, tile), tile)
            part = dotf(mg[b, :, pl.ds(k0, size)], wv[cols, pl.ds(k0, size)], NT)
            if not first:
                part = part + acc[b, :, cols]
            if low:
                part = part + 2.0 * dotf(r_lb[b], bi[b, :, cols], TN)
            if last:
                gv[b, :, cols] = (part * fa[b, :, cols]).astype(jnp.bfloat16)
                uv[b, :, cols] = (part * fb[b, :, cols]).astype(jnp.bfloat16)
            else:
                acc[b, :, cols] = part
            return carry

        lax.fori_loop(0, ftiles, body, 0)

    def close(b):
        def body(j, carry):
            cols = pl.ds(pl.multiple_of(j * tile, tile), tile)
            part = acc[b, :, cols] + 2.0 * dotf(r_lb[b], bi[b, :, cols], TN)
            gv[b, :, cols] = (part * fa[b, :, cols]).astype(jnp.bfloat16)
            uv[b, :, cols] = (part * fb[b, :, cols]).astype(jnp.bfloat16)
            return carry

        lax.fori_loop(0, ftiles, body, 0)

    def sides(step, fn):
        def side(i, carry):
            b = z + step - i * 2 * step

            @pl.when((b >= 0) & (b < n))
            def _():
                fn(b)

            return carry

        lax.fori_loop(0, 2, side, 0)

    def low_back():
        for k in range(1, n):
            arrived(K_AO, s_ao, r_ao, k, "tensor")
        back = jnp.zeros((r_lb.shape[1], BLOCK), jnp.float32)
        for q in range(n):
            back = back + dotf(r_ao[q], mg[z, :, pl.ds(q * feat, feat)], NT)
        r_lb[z] = back.astype(jnp.bfloat16)
        for k in range(1, n):
            small(K_LB, r_lb, r_lb, k, "tensor").start()


    def out_terms():
        for k in range(1, n):
            arrived(K_LI, s_li, r_li, k, "tensor")
        low_in = r_li[0]
        for q in range(1, n):
            low_in = low_in + r_li[q]
        low_in = low_in.astype(jnp.bfloat16)
        for q in range(n):
            s_to[q] = (2.0 * dotf(low_in, mg[z, :, pl.ds(q * feat, feat)])).astype(jnp.bfloat16)
        r_to[z] = s_to[z]
        for k in range(1, n):
            small(K_TO, s_to, r_to, k, "tensor").start()

    def block_of(o):
        index = jnp.int32(0)
        valid = jnp.float32(0.0)
        for b in range(blocks):
            hit = my_slot(b) // owned == o
            index = jnp.where(hit, b, index)
            valid = jnp.where(hit, 1.0, valid)
        return index, valid

    def send_in_terms():
        for o in range(m):
            index, valid = block_of(o)
            lb = r_lb[index]

            def term(j, carry, o=o, lb=lb, index=index, valid=valid):
                cols = pl.ds(pl.multiple_of(j * tile, tile), tile)
                s_gi[o, :, cols] = (
                    (2.0 * valid) * dotf(lb, hid[index, :, cols])
                ).astype(jnp.bfloat16)
                return carry

            lax.fori_loop(0, ftiles, term, 0)
        for k in range(1, m):
            small(K_GIN, s_gi, out_gi, k, "dp").start()
        out_gi[d] = s_gi[d]

    def send_out_terms():
        for k in range(1, n):
            arrived(K_TO, s_to, r_to, k, "tensor")
        for o in range(m):
            index, valid = block_of(o)
            s_go[o] = (r_to[index].astype(jnp.float32) * valid).astype(jnp.bfloat16)
        for k in range(1, m):
            small(K_GOUT, s_go, out_go, k, "dp").start()
        out_go[d] = s_go[d]

    for step in range(1, n):
        final = step == n - 1
        for c in range(chunks):
            poll(step, c)
            if step == 1 and c == 0:
                wload.wait()
                accumulate(z, True, False, False, 0, width)
                low_back()
            if final:
                sides(
                    step,
                    lambda b: accumulate(
                        b, c == 0, c == chunks - 1, c == 0, starts[c], sizes[c]
                    ),
                )
        if step == 1:
            out_terms()
            if not final:
                sides(step, lambda b: accumulate(b, True, False, False, 0, width))
        if step == n - 2:
            for k in range(1, n):
                arrived(K_LB, r_lb, r_lb, k, "tensor")
            send_in_terms()
            close(z)
            sides(1, close)
        if 1 < step < n - 1:
            sides(step, lambda b: accumulate(b, True, True, True, 0, width))
        if step == n - 2:
            send_out_terms()

    for k in range(1, m):
        arrived(K_GIN, s_gi, out_gi, k, "dp")
        arrived(K_GOUT, s_go, out_go, k, "dp")
    for k in range(1, m):
        small(K_AIN, s_in, r_in, k, "dp").wait_send()
        small(K_AOUT, s_out, r_out, k, "dp").wait_send()
        small(K_GIN, s_gi, out_gi, k, "dp").wait_send()
        small(K_GOUT, s_go, out_go, k, "dp").wait_send()
    for k in range(1, n):
        small(K_AO, s_ao, r_ao, k, "tensor").wait_send()
        small(K_LB, r_lb, r_lb, k, "tensor").wait_send()
        small(K_LI, s_li, r_li, k, "tensor").wait_send()
        small(K_TO, s_to, r_to, k, "tensor").wait_send()
    for shard in range(n):
        for c in range(chunks):

            @pl.when((z > 0) & (shard >= z))
            def _():
                piece(0, shard, c).wait_send()

            @pl.when((z < n - 1) & (shard <= z))
            def _():
                piece(1, shard, c).wait_send()


def finish_kernel(m, ids, slot_of, g, u, vi, vo, out_g, out_u, out_gi, out_go, zi, zo, sem):
    d = lax.axis_index("dp")
    owned = out_gi.shape[0]
    blocks = g.shape[0]
    copies = []
    for b in range(blocks):
        rows = pl.ds(b * BLOCK, BLOCK)
        copies.append(pltpu.make_async_copy(g.at[b], out_g.at[rows], sem.at[2 * b]))
        copies.append(pltpu.make_async_copy(u.at[b], out_u.at[rows], sem.at[2 * b + 1]))
    for cp in copies:
        cp.start()
    def clear(s, carry):
        zi[s] = jnp.zeros(zi.shape[1:], zi.dtype)
        zo[s] = jnp.zeros(zo.shape[1:], zo.dtype)
        return carry

    lax.fori_loop(0, owned, clear, 0)
    picks = []
    for e in range(m):
        index = jnp.int32(0)
        hits = jnp.int32(0)
        for b in range(blocks):
            s = slot_of[ids[(e * blocks + b) * BLOCK]]
            hit = s // owned == d
            index = jnp.where(hit, s % owned, index)
            hits = jnp.where(hit, 1, hits)
        picks.append((index, hits > 0))
    for e in range(m):

        @pl.when(picks[e][1])
        def _():
            for src, dst in ((vi, zi), (vo, zo)):
                total = jnp.zeros(src.shape[1:], jnp.float32)
                for f in range(m):
                    same = picks[f][1] & (picks[f][0] == picks[e][0])
                    total = total + jnp.where(same, src[f].astype(jnp.float32), 0.0)
                dst[picks[e][0]] = total.astype(dst.dtype)

    stores = (
        pltpu.make_async_copy(zi, out_gi, sem.at[2 * blocks]),
        pltpu.make_async_copy(zo, out_go, sem.at[2 * blocks + 1]),
    )
    for cp in stores:
        cp.start()
    for cp in stores:
        cp.wait()
    for cp in copies:
        cp.wait()


def fused(
    n,
    m,
    chunks,
    cotangent,
    gate_pre,
    up_pre,
    down_weight,
    adapter_in,
    adapter_out,
    token_adapter,
    live_rows,
    adapter_slot,
):
    tok, ff = gate_pre.shape
    blocks = tok // BLOCK
    cot = cotangent[0]
    width = cot.shape[1]
    owned, rank, feat = adapter_out.shape
    tile = next(t for t in (640, 512, 256, 128) if ff % t == 0)
    bf, f32 = jnp.bfloat16, jnp.float32
    anyspec = pl.BlockSpec(memory_space=pl.ANY)
    smem = pl.BlockSpec(memory_space=pltpu.SMEM)
    vmem = pl.BlockSpec(memory_space=pltpu.VMEM)
    big = max(n, m)
    g, u, gi, go = pl.pallas_call(
        functools.partial(fused_kernel, n, m, chunks, tile),
        out_shape=(
            pltpu.VMEM((blocks, BLOCK, ff), bf),
            pltpu.VMEM((blocks, BLOCK, ff), bf),
            pltpu.VMEM((m, rank, ff), bf),
            pltpu.VMEM((m, rank, feat), bf),
        ),
        in_specs=[smem] * 3 + [anyspec] * 6,
        out_specs=(vmem,) * 4,
        scratch_shapes=[
            pltpu.VMEM((BLOCK, width), bf),
            pltpu.VMEM((n, BLOCK, width), bf),
            pltpu.VMEM(down_weight.shape, bf),
            pltpu.VMEM((blocks, BLOCK, ff), bf),
            pltpu.VMEM((blocks, BLOCK, ff), f32),
            pltpu.VMEM((blocks, BLOCK, ff), f32),
            pltpu.VMEM((blocks, BLOCK, ff), f32),
            pltpu.VMEM(adapter_in.shape, bf),
            pltpu.VMEM(adapter_out.shape, bf),
            pltpu.VMEM((m, rank, ff), bf),
            pltpu.VMEM((m, rank, feat), bf),
            pltpu.VMEM((m, rank, ff), bf),
            pltpu.VMEM((m, rank, feat), bf),
            pltpu.VMEM((blocks, rank, ff), bf),
            pltpu.VMEM((n, rank, feat), bf),
            pltpu.VMEM((n, rank, feat), bf),
            pltpu.VMEM((n, rank, BLOCK), bf),
            pltpu.VMEM((n, rank, BLOCK), f32),
            pltpu.VMEM((n, rank, BLOCK), f32),
            pltpu.VMEM((n, rank, feat), bf),
            pltpu.VMEM((n, rank, feat), bf),
            pltpu.VMEM((m, rank, ff), bf),
            pltpu.VMEM((m, rank, feat), bf),
            pltpu.SemaphoreType.DMA((2, n, len(chunks))),
            pltpu.SemaphoreType.DMA((n, len(chunks))),
            pltpu.SemaphoreType.DMA((8, big)),
            pltpu.SemaphoreType.DMA((8, big)),
            pltpu.SemaphoreType.DMA((4 + 2 * blocks,)),
        ],
        compiler_params=pltpu.CompilerParams(
            collective_id=0, has_side_effects=True, vmem_limit_bytes=VMEM_BYTES
        ),
        name="fused_backward",
    )(
        token_adapter,
        live_rows,
        adapter_slot,
        cot,
        gate_pre,
        up_pre,
        down_weight,
        adapter_in,
        adapter_out,
    )
    return pl.pallas_call(
        functools.partial(finish_kernel, m),
        out_shape=(
            jax.ShapeDtypeStruct((tok, ff), bf),
            jax.ShapeDtypeStruct((tok, ff), bf),
            jax.ShapeDtypeStruct(adapter_in.shape, bf),
            jax.ShapeDtypeStruct(adapter_out.shape, bf),
        ),
        in_specs=[smem] * 2 + [vmem] * 4,
        out_specs=(anyspec,) * 4,
        scratch_shapes=[
            pltpu.VMEM(adapter_in.shape, bf),
            pltpu.VMEM(adapter_out.shape, bf),
            pltpu.SemaphoreType.DMA((2 * blocks + 2,)),
        ],
        compiler_params=pltpu.CompilerParams(vmem_limit_bytes=16 * 2**20),
        name="finish",
    )(token_adapter, adapter_slot, g, u, gi, go)


CHUNKS = (1280, 1024, 256)


def dispatch(*args):
    cotangent, gate_pre, _, _, _, adapter_out = args[:6]
    n, m = lax.axis_size("tensor"), lax.axis_size("dp")
    tok, ff = gate_pre.shape
    aligned = (
        cotangent.shape[1] == BLOCK
        and tok == n * BLOCK
        and ff % 128 == 0
        and adapter_out.shape[2] % 128 == 0
        and cotangent.shape[2] == sum(CHUNKS)
        and n > 2
    )
    if aligned:
        return fused(n, m, CHUNKS, *args)
    return local(*args)


def solution(mesh):
    placed = (
        P("dp", ("groups", "tensor"), None),
        P(("groups", "dp"), "tensor"),
        P(("groups", "dp"), "tensor"),
        P("tensor", None),
        P(("groups", "dp"), None, "tensor"),
        P(("groups", "dp"), None, "tensor"),
        P("groups"),
        P("groups"),
        P("groups"),
    )
    return jax.shard_map(
        dispatch,
        mesh=mesh,
        in_specs=placed,
        out_specs=(
            P(("groups", "dp"), "tensor"),
            P(("groups", "dp"), "tensor"),
            P(("groups", "dp"), None, "tensor"),
            P(("groups", "dp"), None, "tensor"),
        ),
        check_vma=False,
    )
```

```python
import functools

import jax
import jax.numpy as jnp
from jax import lax
from jax.experimental import pallas as pl
from jax.experimental.pallas import tpu as pltpu
from jax.sharding import PartitionSpec as P

BLOCK = 128
SLABS = 4
MESH = pl.DeviceIdType.MESH
NT = (((1,), (1,)), ((), ()))
TN = (((0,), (0,)), ((), ()))
VMEM_BYTES = 53 * 2**20
K_AIN, K_AOUT, K_GIN, K_GOUT, K_AO, K_LB, K_LI, K_TO = range(8)


lowrank_scale_factor = 2.0


def owned_sum(slot_ids, owner_index, owned, terms):
    local_ids = slot_ids % owned
    belongs = slot_ids // owned == owner_index
    selector = (local_ids[None, :] == jnp.arange(owned, dtype=jnp.int32)[:, None]) & belongs[
        None, :
    ]
    flat = terms.reshape(terms.shape[0], -1)
    summed = jnp.dot(
        selector.astype(jnp.float32),
        flat,
        precision=lax.Precision.HIGHEST,
        preferred_element_type=jnp.float32,
    )
    return summed.reshape((owned,) + terms.shape[1:])


def local(
    cotangent,
    gate_pre,
    up_pre,
    down_weight,
    adapter_in,
    adapter_out,
    token_adapter,
    live_rows,
    adapter_slot,
):
    dp_count = lax.axis_size("dp")
    dp_index = lax.axis_index("dp")
    tensor_index = lax.axis_index("tensor")
    tok_rows, ff_local = gate_pre.shape
    width = cotangent.shape[2]
    feat_local = adapter_out.shape[2]
    owned = adapter_in.shape[0]
    blocks = tok_rows // BLOCK
    total_blocks = live_rows.shape[0]
    gathered = lax.all_gather(cotangent, "tensor", axis=1, tiled=True)[0]
    block_ids = token_adapter.reshape(total_blocks, BLOCK)[:, 0]
    adapter_count = adapter_slot.shape[0]
    lookup = block_ids[:, None] == jnp.arange(adapter_count, dtype=jnp.int32)[None, :]
    all_slots = jnp.sum(jnp.where(lookup, adapter_slot[None, :], 0), axis=1)
    my_slots = lax.dynamic_slice_in_dim(all_slots, dp_index * blocks, blocks)
    my_live = lax.dynamic_slice_in_dim(live_rows, dp_index * blocks, blocks)
    slot_grid = all_slots.reshape(dp_count, blocks)
    owner_grid = slot_grid // owned
    my_owner = lax.dynamic_index_in_dim(owner_grid, dp_index, 0, keepdims=False)
    keep = jnp.arange(BLOCK, dtype=jnp.int32)[None, :] < my_live[:, None]
    masked = jnp.where(keep.reshape(tok_rows, 1), gathered, jnp.zeros((), jnp.bfloat16))
    gate_val = gate_pre.astype(jnp.float32)
    up_val = up_pre.astype(jnp.float32)
    sigma = jax.nn.sigmoid(gate_val)
    hidden = (gate_val * sigma * up_val).astype(jnp.bfloat16)
    every_in, every_out = (
        lax.all_gather(adapter_in, "dp", axis=0, tiled=True),
        lax.all_gather(adapter_out, "dp", axis=0, tiled=True),
    )
    block_in = every_in[my_slots]
    block_out = every_out[my_slots]
    hidden_block_rows = hidden.reshape(blocks, BLOCK, ff_local)
    masked_block_rows = masked.reshape(blocks, BLOCK, width)
    masked_local = lax.dynamic_slice_in_dim(
        masked_block_rows, tensor_index * feat_local, feat_local, 2
    )
    part_in = jnp.einsum(
        "bnf,brf->bnr", hidden_block_rows, block_in, preferred_element_type=jnp.float32
    )
    part_back = jnp.einsum(
        "bnd,brd->bnr", masked_local, block_out, preferred_element_type=jnp.float32
    )
    lowrank_input, lowrank_gradient = lax.psum((part_in, part_back), "tensor")
    lowrank_input = lowrank_input.astype(jnp.bfloat16)
    lowrank_gradient = lowrank_gradient.astype(jnp.bfloat16)
    frozen_output = lax.dot_general(
        masked, down_weight, (((1,), (1,)), ((), ())), preferred_element_type=jnp.float32
    )
    adapter_applied = jnp.einsum(
        "bnr,brf->bnf", lowrank_gradient, block_in, preferred_element_type=jnp.float32
    ).reshape(tok_rows, ff_local)
    hidden_gradient = frozen_output + lowrank_scale_factor * adapter_applied
    gate_grad = (hidden_gradient * up_val * sigma * (1.0 + gate_val * (1.0 - sigma))).astype(
        jnp.bfloat16
    )
    up_grad = (hidden_gradient * gate_val * sigma).astype(jnp.bfloat16)
    incoming_terms = lowrank_scale_factor * jnp.einsum(
        "oqx,oqg->oxg", lowrank_gradient, hidden_block_rows, preferred_element_type=jnp.float32
    )
    outgoing_terms = lowrank_scale_factor * jnp.einsum(
        "ykx,ykz->yxz", lowrank_input, masked_local, preferred_element_type=jnp.float32
    )
    route = my_owner[None, :] == jnp.arange(dp_count, dtype=jnp.int32)[:, None]
    send_terms_in = jnp.where(route[:, :, None, None], incoming_terms[None], 0.0)
    send_terms_out = jnp.where(route[:, :, None, None], outgoing_terms[None], 0.0)
    got_terms_in, got_terms_out = (
        lax.all_to_all(send_terms_in, "dp", split_axis=0, concat_axis=0, tiled=True),
        lax.all_to_all(send_terms_out, "dp", split_axis=0, concat_axis=0, tiled=True),
    )
    grad_in = owned_sum(
        all_slots,
        dp_index,
        owned,
        got_terms_in.reshape((dp_count * blocks,) + incoming_terms.shape[1:]),
    )
    grad_out = owned_sum(
        all_slots,
        dp_index,
        owned,
        got_terms_out.reshape((dp_count * blocks,) + outgoing_terms.shape[1:]),
    )
    return (gate_grad, up_grad, grad_in.astype(jnp.bfloat16), grad_out.astype(jnp.bfloat16))


def dotf(a, b, dims=(((1,), (0,)), ((), ()))):
    return lax.dot_general(a, b, dims, preferred_element_type=jnp.float32)


def fused_kernel(
    n,
    m,
    chunk_sizes,
    tile,
    ids,
    live,
    slot_of,
    cot,
    gate,
    up,
    weight,
    ain,
    aout,
    gv,
    uv,
    out_gi,
    out_go,
    cotv,
    mg,
    wt,
    stage,
    hid,
    fa,
    fb,
    acc,
    aiv,
    aov,
    s_in,
    s_out,
    r_in,
    r_out,
    bi,
    s_ao,
    r_ao,
    r_lb,
    s_li,
    r_li,
    s_to,
    r_to,
    s_gi,
    s_go,
    gsend,
    grecv,
    ssend,
    srecv,
    lsem,
    wsem,
):
    z = lax.axis_index("tensor")
    d = lax.axis_index("dp")
    width = cot.shape[1]
    feat = aov.shape[2]
    ff = gate.shape[1]
    owned = aov.shape[0]
    blocks = gv.shape[0]
    sizes = chunk_sizes
    starts = [sum(sizes[:i]) for i in range(len(sizes))]
    chunks = len(sizes)
    ftiles = ff // tile

    loads = [
        pltpu.make_async_copy(cot, cotv, lsem.at[0]),
        pltpu.make_async_copy(aout, aov, lsem.at[1]),
        pltpu.make_async_copy(ain, aiv, lsem.at[2]),
    ]
    gu = []
    for b in range(blocks):
        rows = pl.ds(b * BLOCK, BLOCK)
        gu.append(
            (
                pltpu.make_async_copy(gate.at[rows], gv.at[b], lsem.at[4 + 2 * b]),
                pltpu.make_async_copy(up.at[rows], uv.at[b], lsem.at[5 + 2 * b]),
            )
        )
    slabs = ff // BLOCK

    def slab(i):
        place = lax.rem(i, SLABS)
        rows = pl.ds(pl.multiple_of(i * BLOCK, BLOCK), BLOCK)
        return pltpu.make_async_copy(weight.at[rows], stage.at[place], wsem.at[place])

    for c in loads:
        c.start()

    def slot(block):
        return slot_of[ids[block * BLOCK]]

    def my_slot(b):
        return slot(d * blocks + b)

    barrier = pltpu.get_barrier_semaphore()
    for k in range(1, n):
        pl.semaphore_signal(
            barrier, inc=1, device_id={"tensor": lax.rem(z + k, n)}, device_id_type=MESH
        )
    for k in range(1, m):
        pl.semaphore_signal(
            barrier, inc=1, device_id={"dp": lax.rem(d + k, m)}, device_id_type=MESH
        )
    pl.semaphore_wait(barrier, n - 1 + m - 1)

    def piece(direction, shard, c):
        part = mg.at[shard, :, pl.ds(starts[c], sizes[c])]
        return pltpu.make_async_remote_copy(
            src_ref=part,
            dst_ref=part,
            send_sem=gsend.at[direction, shard, c],
            recv_sem=grecv.at[shard, c],
            device_id={"tensor": z - 1 if direction == 0 else z + 1},
            device_id_type=MESH,
        )

    def small(kind, src, dst, k, axis):
        me, size = (z, n) if axis == "tensor" else (d, m)
        peer = lax.rem(me + k, size)
        return pltpu.make_async_remote_copy(
            src_ref=src.at[peer] if src is not dst else src.at[me],
            dst_ref=dst.at[me],
            send_sem=ssend.at[kind, peer],
            recv_sem=srecv.at[kind, me],
            device_id={axis: peer},
            device_id_type=MESH,
        )

    def arrived(kind, src, dst, k, axis):
        me, size = (z, n) if axis == "tensor" else (d, m)
        frm = lax.rem(me + k, size)
        pltpu.make_async_remote_copy(
            src_ref=src.at[frm],
            dst_ref=dst.at[frm],
            send_sem=ssend.at[kind, frm],
            recv_sem=srecv.at[kind, frm],
            device_id={axis: frm},
            device_id_type=MESH,
        ).wait_recv()

    loads[0].wait()
    count = live[d * blocks + z]
    for c in range(chunks):
        cols = pl.ds(starts[c], sizes[c])
        keep = lax.broadcasted_iota(jnp.int32, (BLOCK, sizes[c]), 0) < count
        val = cotv[:, cols].astype(jnp.float32)
        mg[z, :, cols] = jnp.where(keep, val, 0.0).astype(jnp.bfloat16)
        for direction in range(2):

            @pl.when(z > 0 if direction == 0 else z < n - 1)
            def _():
                piece(direction, z, c).start()

    for pair in gu:
        pair[0].start()
        pair[1].start()
    for i in range(SLABS):
        slab(jnp.int32(i)).start()

    loads[1].wait()
    loads[2].wait()
    for e in range(m):
        index = jnp.int32(0)
        for b in range(blocks):
            s = slot(e * blocks + b)
            index = jnp.where(s // owned == d, s % owned, index)
        s_out[e] = aov[index]
        s_in[e] = aiv[index]
    for k in range(1, m):
        small(K_AOUT, s_out, r_out, k, "dp").start()
    for k in range(1, m):
        small(K_AIN, s_in, r_in, k, "dp").start()
    r_out[d] = s_out[d]
    r_in[d] = s_in[d]

    for b in range(blocks):
        gu[b][0].wait()
        gu[b][1].wait()

        def row_group(i, carry, b=b):
            rows = pl.ds(pl.multiple_of(i * 16, 16), 16)
            for j in range(ftiles):
                cols = pl.ds(j * tile, tile)
                g = gv[b, rows, cols].astype(jnp.float32)
                u = uv[b, rows, cols].astype(jnp.float32)
                s = jax.nn.sigmoid(g)
                gs = g * s
                hid[b, rows, cols] = (gs * u).astype(jnp.bfloat16)
                fb[b, rows, cols] = gs
                fa[b, rows, cols] = u * s * (1.0 + g * (1.0 - s))
            return carry

        lax.fori_loop(0, BLOCK // 16, row_group, 0)

    for k in range(1, m):
        arrived(K_AIN, s_in, r_in, k, "dp")
    for b in range(blocks):
        bi[b] = r_in[my_slot(b) // owned]
        s_li[b] = dotf(bi[b], hid[b], NT)
    r_li[z] = s_li[z]
    for k in range(1, n):
        small(K_LI, s_li, r_li, k, "tensor").start()

    for k in range(1, m):
        arrived(K_AOUT, s_out, r_out, k, "dp")
    for b in range(n):
        s_ao[b] = r_out[my_slot(b) // owned]
    r_ao[z] = s_ao[z]
    for k in range(1, n):
        small(K_AO, s_ao, r_ao, k, "tensor").start()

    def poll(step, c):
        @pl.when(z + step < n)
        def _():
            piece(0, z + step, c).wait_recv()

            @pl.when(z > 0)
            def _():
                piece(0, z + step, c).start()

        @pl.when(z - step >= 0)
        def _():
            piece(1, z - step, c).wait_recv()

            @pl.when(z < n - 1)
            def _():
                piece(1, z - step, c).start()

    def accumulate(b, first, last, low, k0, size):
        for j in range(0, ff, 2 * tile):
            cols = pl.ds(j, min(2 * tile, ff - j))
            part = dotf(mg[b, :, pl.ds(k0, size)], wt[pl.ds(k0, size), cols])
            if not first:
                part = part + acc[b, :, cols]
            if low:
                part = part + 2.0 * dotf(r_lb[b], bi[b, :, cols], TN)
            if last:
                gv[b, :, cols] = (part * fa[b, :, cols]).astype(jnp.bfloat16)
                uv[b, :, cols] = (part * fb[b, :, cols]).astype(jnp.bfloat16)
            else:
                acc[b, :, cols] = part

    def close(b):
        def body(j, carry):
            cols = pl.ds(pl.multiple_of(j * tile, tile), tile)
            part = acc[b, :, cols] + 2.0 * dotf(r_lb[b], bi[b, :, cols], TN)
            gv[b, :, cols] = (part * fa[b, :, cols]).astype(jnp.bfloat16)
            uv[b, :, cols] = (part * fb[b, :, cols]).astype(jnp.bfloat16)
            return carry

        lax.fori_loop(0, ftiles, body, 0)

    def sides(step, fn):
        def side(i, carry):
            b = z + step - i * 2 * step

            @pl.when((b >= 0) & (b < n))
            def _():
                fn(b)

            return carry

        lax.fori_loop(0, 2, side, 0)

    def low_back():
        for k in range(1, n):
            arrived(K_AO, s_ao, r_ao, k, "tensor")
        back = jnp.zeros((r_lb.shape[1], BLOCK), jnp.float32)
        for q in range(n):
            back = back + dotf(r_ao[q], mg[z, :, pl.ds(q * feat, feat)], NT)
        r_lb[z] = back.astype(jnp.bfloat16)
        for k in range(1, n):
            small(K_LB, r_lb, r_lb, k, "tensor").start()


    def out_terms():
        for k in range(1, n):
            arrived(K_LI, s_li, r_li, k, "tensor")
        low_in = r_li[0]
        for q in range(1, n):
            low_in = low_in + r_li[q]
        low_in = low_in.astype(jnp.bfloat16)
        for q in range(n):
            s_to[q] = (2.0 * dotf(low_in, mg[z, :, pl.ds(q * feat, feat)])).astype(jnp.bfloat16)
        r_to[z] = s_to[z]
        for k in range(1, n):
            small(K_TO, s_to, r_to, k, "tensor").start()

    def block_of(o):
        index = jnp.int32(0)
        valid = jnp.float32(0.0)
        for b in range(blocks):
            hit = my_slot(b) // owned == o
            index = jnp.where(hit, b, index)
            valid = jnp.where(hit, 1.0, valid)
        return index, valid

    def send_in_terms():
        for o in range(m):
            index, valid = block_of(o)
            lb = r_lb[index]

            def term(j, carry, o=o, lb=lb, index=index, valid=valid):
                cols = pl.ds(pl.multiple_of(j * tile, tile), tile)
                s_gi[o, :, cols] = (
                    (2.0 * valid) * dotf(lb, hid[index, :, cols])
                ).astype(jnp.bfloat16)
                return carry

            lax.fori_loop(0, ftiles, term, 0)
        for k in range(1, m):
            small(K_GIN, s_gi, out_gi, k, "dp").start()
        out_gi[d] = s_gi[d]

    def send_out_terms():
        for k in range(1, n):
            arrived(K_TO, s_to, r_to, k, "tensor")
        for o in range(m):
            index, valid = block_of(o)
            s_go[o] = (r_to[index].astype(jnp.float32) * valid).astype(jnp.bfloat16)
        for k in range(1, m):
            small(K_GOUT, s_go, out_go, k, "dp").start()
        out_go[d] = s_go[d]

    for step in range(1, n):
        final = step == n - 1
        for c in range(chunks):
            poll(step, c)
            if step == 1 and c == 0:

                def turn(i, carry):
                    slab(i).wait()
                    cols = pl.ds(pl.multiple_of(i * BLOCK, BLOCK), BLOCK)
                    wt[:, cols] = stage[lax.rem(i, SLABS)].T

                    @pl.when(i + SLABS < slabs)
                    def _():
                        slab(i + SLABS).start()

                    return carry

                lax.fori_loop(0, slabs, turn, 0)
                accumulate(z, True, False, False, 0, width)
                low_back()
            if final:
                sides(
                    step,
                    lambda b: accumulate(
                        b, c == 0, c == chunks - 1, c == 0, starts[c], sizes[c]
                    ),
                )
        if step == 1:
            out_terms()
            if not final:
                sides(step, lambda b: accumulate(b, True, False, False, 0, width))
        if step == n - 2:
            for k in range(1, n):
                arrived(K_LB, r_lb, r_lb, k, "tensor")
            send_in_terms()
            close(z)
            sides(1, close)
        if 1 < step < n - 1:
            sides(step, lambda b: accumulate(b, True, True, True, 0, width))
        if step == n - 2:
            send_out_terms()

    for k in range(1, m):
        arrived(K_GIN, s_gi, out_gi, k, "dp")
        arrived(K_GOUT, s_go, out_go, k, "dp")
    for k in range(1, m):
        small(K_AIN, s_in, r_in, k, "dp").wait_send()
        small(K_AOUT, s_out, r_out, k, "dp").wait_send()
        small(K_GIN, s_gi, out_gi, k, "dp").wait_send()
        small(K_GOUT, s_go, out_go, k, "dp").wait_send()
    for k in range(1, n):
        small(K_AO, s_ao, r_ao, k, "tensor").wait_send()
        small(K_LB, r_lb, r_lb, k, "tensor").wait_send()
        small(K_LI, s_li, r_li, k, "tensor").wait_send()
        small(K_TO, s_to, r_to, k, "tensor").wait_send()
    for shard in range(n):
        for c in range(chunks):

            @pl.when((z > 0) & (shard >= z))
            def _():
                piece(0, shard, c).wait_send()

            @pl.when((z < n - 1) & (shard <= z))
            def _():
                piece(1, shard, c).wait_send()


def finish_kernel(m, ids, slot_of, g, u, vi, vo, out_g, out_u, out_gi, out_go, zi, zo, sem):
    d = lax.axis_index("dp")
    owned = out_gi.shape[0]
    blocks = g.shape[0]
    copies = []
    for b in range(blocks):
        rows = pl.ds(b * BLOCK, BLOCK)
        copies.append(pltpu.make_async_copy(g.at[b], out_g.at[rows], sem.at[2 * b]))
        copies.append(pltpu.make_async_copy(u.at[b], out_u.at[rows], sem.at[2 * b + 1]))
    for cp in copies:
        cp.start()
    def clear(s, carry):
        zi[s] = jnp.zeros(zi.shape[1:], zi.dtype)
        zo[s] = jnp.zeros(zo.shape[1:], zo.dtype)
        return carry

    lax.fori_loop(0, owned, clear, 0)
    picks = []
    for e in range(m):
        index = jnp.int32(0)
        hits = jnp.int32(0)
        for b in range(blocks):
            s = slot_of[ids[(e * blocks + b) * BLOCK]]
            hit = s // owned == d
            index = jnp.where(hit, s % owned, index)
            hits = jnp.where(hit, 1, hits)
        picks.append((index, hits > 0))
    for e in range(m):

        @pl.when(picks[e][1])
        def _():
            for src, dst in ((vi, zi), (vo, zo)):
                total = jnp.zeros(src.shape[1:], jnp.float32)
                for f in range(m):
                    same = picks[f][1] & (picks[f][0] == picks[e][0])
                    total = total + jnp.where(same, src[f].astype(jnp.float32), 0.0)
                dst[picks[e][0]] = total.astype(dst.dtype)

    stores = (
        pltpu.make_async_copy(zi, out_gi, sem.at[2 * blocks]),
        pltpu.make_async_copy(zo, out_go, sem.at[2 * blocks + 1]),
    )
    for cp in stores:
        cp.start()
    for cp in stores:
        cp.wait()
    for cp in copies:
        cp.wait()


def fused(
    n,
    m,
    chunks,
    cotangent,
    gate_pre,
    up_pre,
    down_weight,
    adapter_in,
    adapter_out,
    token_adapter,
    live_rows,
    adapter_slot,
):
    tok, ff = gate_pre.shape
    blocks = tok // BLOCK
    cot = cotangent[0]
    width = cot.shape[1]
    owned, rank, feat = adapter_out.shape
    tile = next(t for t in (640, 512, 256, 128) if ff % t == 0)
    bf, f32 = jnp.bfloat16, jnp.float32
    anyspec = pl.BlockSpec(memory_space=pl.ANY)
    smem = pl.BlockSpec(memory_space=pltpu.SMEM)
    vmem = pl.BlockSpec(memory_space=pltpu.VMEM)
    big = max(n, m)
    g, u, gi, go = pl.pallas_call(
        functools.partial(fused_kernel, n, m, chunks, tile),
        out_shape=(
            pltpu.VMEM((blocks, BLOCK, ff), bf),
            pltpu.VMEM((blocks, BLOCK, ff), bf),
            pltpu.VMEM((m, rank, ff), bf),
            pltpu.VMEM((m, rank, feat), bf),
        ),
        in_specs=[smem] * 3 + [anyspec] * 6,
        out_specs=(vmem,) * 4,
        scratch_shapes=[
            pltpu.VMEM((BLOCK, width), bf),
            pltpu.VMEM((n, BLOCK, width), bf),
            pltpu.VMEM((width, ff), bf),
            pltpu.VMEM((SLABS, BLOCK, width), bf),
            pltpu.VMEM((blocks, BLOCK, ff), bf),
            pltpu.VMEM((blocks, BLOCK, ff), f32),
            pltpu.VMEM((blocks, BLOCK, ff), f32),
            pltpu.VMEM((blocks, BLOCK, ff), f32),
            pltpu.VMEM(adapter_in.shape, bf),
            pltpu.VMEM(adapter_out.shape, bf),
            pltpu.VMEM((m, rank, ff), bf),
            pltpu.VMEM((m, rank, feat), bf),
            pltpu.VMEM((m, rank, ff), bf),
            pltpu.VMEM((m, rank, feat), bf),
            pltpu.VMEM((blocks, rank, ff), bf),
            pltpu.VMEM((n, rank, feat), bf),
            pltpu.VMEM((n, rank, feat), bf),
            pltpu.VMEM((n, rank, BLOCK), bf),
            pltpu.VMEM((n, rank, BLOCK), f32),
            pltpu.VMEM((n, rank, BLOCK), f32),
            pltpu.VMEM((n, rank, feat), bf),
            pltpu.VMEM((n, rank, feat), bf),
            pltpu.VMEM((m, rank, ff), bf),
            pltpu.VMEM((m, rank, feat), bf),
            pltpu.SemaphoreType.DMA((2, n, len(chunks))),
            pltpu.SemaphoreType.DMA((n, len(chunks))),
            pltpu.SemaphoreType.DMA((8, big)),
            pltpu.SemaphoreType.DMA((8, big)),
            pltpu.SemaphoreType.DMA((4 + 2 * blocks,)),
            pltpu.SemaphoreType.DMA((SLABS,)),
        ],
        compiler_params=pltpu.CompilerParams(
            collective_id=0, has_side_effects=True, vmem_limit_bytes=VMEM_BYTES
        ),
        name="fused_backward",
    )(
        token_adapter,
        live_rows,
        adapter_slot,
        cot,
        gate_pre,
        up_pre,
        down_weight,
        adapter_in,
        adapter_out,
    )
    return pl.pallas_call(
        functools.partial(finish_kernel, m),
        out_shape=(
            jax.ShapeDtypeStruct((tok, ff), bf),
            jax.ShapeDtypeStruct((tok, ff), bf),
            jax.ShapeDtypeStruct(adapter_in.shape, bf),
            jax.ShapeDtypeStruct(adapter_out.shape, bf),
        ),
        in_specs=[smem] * 2 + [vmem] * 4,
        out_specs=(anyspec,) * 4,
        scratch_shapes=[
            pltpu.VMEM(adapter_in.shape, bf),
            pltpu.VMEM(adapter_out.shape, bf),
            pltpu.SemaphoreType.DMA((2 * blocks + 2,)),
        ],
        compiler_params=pltpu.CompilerParams(vmem_limit_bytes=16 * 2**20),
        name="finish",
    )(token_adapter, adapter_slot, g, u, gi, go)


CHUNKS = (1280, 768, 512)


def dispatch(*args):
    cotangent, gate_pre, _, _, _, adapter_out = args[:6]
    n, m = lax.axis_size("tensor"), lax.axis_size("dp")
    tok, ff = gate_pre.shape
    aligned = (
        cotangent.shape[1] == BLOCK
        and tok == n * BLOCK
        and ff % 128 == 0
        and adapter_out.shape[2] % 128 == 0
        and cotangent.shape[2] == sum(CHUNKS)
        and n > 2
        and ff >= SLABS * BLOCK
    )
    if aligned:
        return fused(n, m, CHUNKS, *args)
    return local(*args)


def solution(mesh):
    placed = (
        P("dp", ("groups", "tensor"), None),
        P(("groups", "dp"), "tensor"),
        P(("groups", "dp"), "tensor"),
        P("tensor", None),
        P(("groups", "dp"), None, "tensor"),
        P(("groups", "dp"), None, "tensor"),
        P("groups"),
        P("groups"),
        P("groups"),
    )
    return jax.shard_map(
        dispatch,
        mesh=mesh,
        in_specs=placed,
        out_specs=(
            P(("groups", "dp"), "tensor"),
            P(("groups", "dp"), "tensor"),
            P(("groups", "dp"), None, "tensor"),
            P(("groups", "dp"), None, "tensor"),
        ),
        check_vma=False,
    )
```
